512 devices in a mesh: leaf: 512 (over x, y, z, core).
Axes of the slice: x: 4, y: 8, z: 8, core: 2. Of those that a mesh axis runs over, the one named last changes fastest.
Arguments:
- features: bfloat16 [262144, 1024], P('leaf'), may hold values from -6 to 6
- probes: float32 [262144, 128], P('leaf'), may hold values from -6 to 6
- bases: float32 [262144, 256], P('leaf'), may hold values from -0.25 to 0.25
- transfers: float32 [512, 4, 256, 256], P('leaf'), may hold values from -1 to 1, as said below
- couplings: float32 [512, 5, 256, 256], P('leaf'), may hold values from -1 to 1, as said below
- near_list: int32 [512, 4], P('leaf'), may hold values from 0 to 511, as said below
- near_count: int32 [512], P('leaf'), may hold values from 1 to 4
Outputs:
- product: float32 [262144, 128], P('leaf')
The draws below stay inside these ranges and needn't reach their ends.
Inputs may be any that keep to these rules, and one draw needn't show every extreme that they name: `near_list`: the first near_count[i] entries of row i are distinct leaves other than i, each at most 2 from i; the other entries equal i. Some leaf lists 4 leaves. transfers[i, l] is the same for all leaves i of one node of level l (an aligned block of 2^l leaves). couplings[i, l] is the same for all leaves i of one node of level l (an aligned block of 2^l leaves).
All inputs are finite; a program needn't handle non-finite values.
Results may differ from the reference program's by a relative error of at most 0.00095.
Values may be sent and summed in bfloat16 or wider, within the bound.
A program may use at most 64 MiB of HBM per device.

```python
import jax
import jax.numpy as jnp
from jax import lax

ROWS = 512
F = 1024
R = 256
P_SIZE = 128
LEV = 4
SPAN = 2
NEAR_MAX = 4
LEAVES = 512
POINTS = 262144


def near_tables(key):
    span_offsets = jnp.concatenate([jnp.arange(-SPAN, 0), jnp.arange(1, SPAN + 1)]).astype(jnp.int32)
    leaf_ids = jnp.arange(LEAVES, dtype=jnp.int32)
    targets = leaf_ids[:, None] + span_offsets[None, :]
    is_valid = (targets >= 0) & (targets < LEAVES)
    score_key = jax.random.fold_in(key, 11)
    count_key = jax.random.fold_in(key, 12)
    slot_ids = jnp.arange(NEAR_MAX, dtype=jnp.int32)
    scores = jax.random.randint(score_key, (LEAVES, NEAR_MAX), 0, 1 << 16) * NEAR_MAX + slot_ids[None, :]
    scores = jnp.where(is_valid, scores, (1 << 28) + slot_ids[None, :])
    ordering = jnp.argsort(scores, axis=1, stable=True)
    listed = jnp.take_along_axis(targets, ordering, axis=1)
    valid_count = jnp.sum(is_valid.astype(jnp.int32), axis=1)
    wanted = jax.random.randint(count_key, (LEAVES,), 1, NEAR_MAX + 1)
    counts = jnp.minimum(wanted, valid_count)
    counts = jnp.where(leaf_ids == LEAVES // 2, NEAR_MAX, counts)
    listed = jnp.where(slot_ids[None, :] < counts[:, None], listed, leaf_ids[:, None])
    return (listed.astype(jnp.int32), counts.astype(jnp.int32))


def draw_near_list(key, part):
    return near_tables(key)[0]


def draw_near_count(key, part):
    return near_tables(key)[1]


def node_matrices(key, level_count):
    stacked = []
    for height in range(level_count):
        level_key = jax.random.fold_in(key, 100 + height)
        drawn = jax.random.uniform(level_key, (LEAVES // 2 ** height, R, R), jnp.float32, -1.0, 1.0)
        stacked.append(jnp.repeat(drawn, 2 ** height, axis=0))
    return jnp.stack(stacked, axis=1)


def draw_transfers(key, part):
    return node_matrices(jax.random.fold_in(key, 21), LEV)


def draw_couplings(key, part):
    return node_matrices(jax.random.fold_in(key, 22), LEV + 1)


def shard_levels(rng, dims, split, low, high):
    level, own = 1.0, jax.random.fold_in(rng, 6)
    for axis_at, shards_of in split:
        draws = jnp.exp(jax.random.uniform(jax.random.fold_in(own, axis_at), (shards_of,), jnp.float32, low / len(split), high / len(split)))
        level = level * jnp.repeat(draws, dims[axis_at] // shards_of).reshape([-1 if axis == axis_at else 1 for axis in range(len(dims))])
    return level


def noise(stream_key, shape, deviation, reach, cuts=(), kind=jnp.bfloat16):
    values = deviation * jax.random.normal(stream_key, shape, jnp.float32)
    if cuts:
        values = values * shard_levels(stream_key, shape, cuts, -0.22, 0.18)
    return jnp.clip(values, -reach, reach).astype(kind)


def setup_inputs(seed: int = 0) -> dict:
    key_of = jax.random.split(jax.random.key(seed), 8)
    return {
        "features": noise(key_of[0], (POINTS, F), 1.0, 6.0, ((0, 512),)),
        "probes": noise(key_of[1], (POINTS, P_SIZE), 1.0, 6.0, ((0, 512),), jnp.float32),
        "bases": noise(key_of[2], (POINTS, R), ROWS ** -0.5, 0.25, ((0, 512),), jnp.float32),
        "transfers": draw_transfers(jax.random.fold_in(key_of[7], 71), 0),
        "couplings": draw_couplings(jax.random.fold_in(key_of[7], 71), 0),
        "near_list": draw_near_list(jax.random.fold_in(key_of[7], 71), 0),
        "near_count": draw_near_count(jax.random.fold_in(key_of[7], 71), 0),
    }


def kernel_tile(rows_a, rows_b):
    gram_tile = jnp.dot(rows_a, rows_b.T, preferred_element_type=jnp.float32)
    return gram_tile * gram_tile * (1.0 / (F * ROWS))


def sibling(values, height):
    half_block = 2 ** height
    grouped = values.reshape(LEAVES // (2 * half_block), 2, half_block, R, P_SIZE)
    return grouped[:, ::-1].reshape(LEAVES, R, P_SIZE)


def reference(features, probes, bases, transfers, couplings, near_list, near_count):
    highest = lax.Precision.HIGHEST
    scale_g = (3.0 / R) ** 0.5
    leaf_features = features.reshape(LEAVES, ROWS, F)
    leaf_probes = probes.reshape(LEAVES, ROWS, P_SIZE)
    padded_features = jnp.concatenate([leaf_features, jnp.zeros((SPAN, ROWS, F), features.dtype)], 0)
    padded_probes = jnp.concatenate([leaf_probes, jnp.zeros((SPAN, ROWS, P_SIZE), jnp.float32)], 0)
    leaf_ids = jnp.arange(LEAVES, dtype=jnp.int32)
    slot_ids = jnp.arange(NEAR_MAX, dtype=jnp.int32)
    is_live = slot_ids[None, :] < near_count[:, None]

    def member(offset):
        found = (near_list == (leaf_ids + offset)[:, None]) & is_live
        return jnp.any(found, axis=1).astype(jnp.float32)

    def per_leaf(leaf_id):
        own_rows = leaf_features[leaf_id]
        own_probes = leaf_probes[leaf_id]
        outputs = [jnp.dot(kernel_tile(own_rows, own_rows), own_probes, precision=highest, preferred_element_type=jnp.float32)]
        for offset in range(1, SPAN + 1):
            remote = lax.dynamic_index_in_dim(padded_features, leaf_id + offset, 0, keepdims=False)
            remote_x = lax.dynamic_index_in_dim(padded_probes, leaf_id + offset, 0, keepdims=False)
            kernel = kernel_tile(own_rows, remote)
            outputs.append(jnp.dot(kernel, remote_x, precision=highest, preferred_element_type=jnp.float32))
            outputs.append(jnp.dot(kernel.T, own_probes, precision=highest, preferred_element_type=jnp.float32))
        return jnp.stack(outputs)

    pieces = lax.map(per_leaf, leaf_ids)
    near_sum = pieces[:, 0]
    for offset in range(1, SPAN + 1):
        near_sum = near_sum + member(offset)[:, None, None] * pieces[:, 2 * offset - 1]
        back_term = pieces[:, 2 * offset]
        shifted = jnp.concatenate([jnp.zeros((offset, ROWS, P_SIZE), jnp.float32), back_term[:LEAVES - offset]], 0)
        near_sum = near_sum + member(-offset)[:, None, None] * shifted

    leaf_bases = bases.reshape(LEAVES, ROWS, R)
    skeleton = jnp.einsum('nra,nrp->nap', leaf_bases, leaf_probes, precision=highest)
    levels = [skeleton]
    for height in range(1, LEV + 1):
        factor = scale_g * 2.0 ** (-0.5 * height)
        contrib = factor * jnp.einsum('nab,nap->nbp', transfers[:, height - 1], levels[-1], precision=highest)
        levels.append(contrib + sibling(contrib, height - 1))

    expansion = scale_g * jnp.einsum('nab,nbp->nap', couplings[:, LEV], sibling(levels[LEV], LEV), precision=highest)
    for height in range(LEV - 1, -1, -1):
        factor = scale_g * 2.0 ** (-0.5 * (height + 1))
        expansion = scale_g * jnp.einsum('nab,nbp->nap', couplings[:, height], sibling(levels[height], height), precision=highest) + factor * jnp.einsum('nab,nbp->nap', transfers[:, height], expansion, precision=highest)
    far_sum = jnp.einsum('nra,nap->nrp', leaf_bases, expansion, precision=highest)
    return (near_sum + far_sum).reshape(LEAVES * ROWS, P_SIZE)
```

```python
import functools

import jax
import jax.numpy as jnp
from jax import lax
from jax.experimental import pallas as pl
from jax.experimental.pallas import tpu as pltpu
from jax.sharding import PartitionSpec as P

F32, BF16 = jnp.float32, jnp.bfloat16
MESH = pl.DeviceIdType.MESH
CHUNKS = 4

NN = (((1,), (0,)), ((), ()))
NT = (((1,), (1,)), ((), ()))
TN = (((0,), (0,)), ((), ()))


def dot(a, b, dims=NN):
    return lax.dot_general(a, b, dims, preferred_element_type=F32)


def split(a):
    high = a.astype(BF16)
    return high, (a - high.astype(F32)).astype(BF16)


def dot3(a, b, dims=NN):
    (ah, al), (bh, bl) = split(a), split(b)
    return dot(ah, bh, dims) + (dot(ah, bl, dims) + dot(al, bh, dims))


def kernel(n, feat, prob, base, tran, coup, nlist, ncount, out,
           phi_q, phi_p, phi_g, phi_o, x_q, x_o, x_cat, x_b, x_p, x_g, u, tm, km,
           s0, s0_r, t1, t1_r, ts, ts_r, ss, ss_r, e1, e1_r, bk, bk_r, acc,
           ld_sem, snd, rcv):
    me = lax.axis_index("leaf")
    core = lax.rem(me, 2)
    rows, feats = phi_q.shape
    ranks = u.shape[1]
    half = x_q.shape[1] // 2
    size = rows // CHUNKS
    g = (3.0 / ranks) ** 0.5
    scale = 1.0 / (feats * rows)
    other = me + 1 - 2 * core
    source = lax.rem(me + n + 2 - 4 * core, n)
    target = lax.rem(me + n - 2 + 4 * core, n)
    sib = [other] + [me + (1 << h) - (2 << h) * lax.rem(me // (1 << h), 2) for h in range(1, 5)]

    def load(src, dst, at):
        copy = pltpu.make_async_copy(src, dst, ld_sem.at[at])
        copy.start()
        return copy

    ld_x = load(prob, x_q, 0)
    ld_u = load(base, u, 1)
    ld_t = load(tran, tm, 2)
    ld_phi = load(feat, phi_q, 3)
    ld_k = load(coup, km, 4)

    barrier = pltpu.get_barrier_semaphore()
    partners = [other, source, target, sib[2], sib[3], sib[4]]
    for p in partners:
        pl.semaphore_signal(barrier, inc=1, device_id=(p,), device_id_type=MESH)
    pl.semaphore_wait(barrier, len(partners))

    count = [0]

    def send(src, dst, to):
        at = count[0]
        count[0] += 1
        copy = pltpu.make_async_remote_copy(
            src_ref=src, dst_ref=dst, send_sem=snd.at[at], recv_sem=rcv.at[at],
            device_id=(to,), device_id_type=MESH)
        copy.start()
        return copy

    def block(k):
        return pl.ds(k * size, size)

    phi_copies = [send(feat.at[block(k)], phi_p.at[block(k)], target) for k in range(CHUNKS)]
    o_copy = send(feat, phi_o, other)
    xo_copy = send(prob, x_o, other)

    ld_x.wait()
    xh, xl = split(x_q[...])
    x_b[...] = xh
    x_copy = send(x_b, x_p, target)
    x_cat[:, :2 * half] = xh
    x_cat[:, 2 * half:] = xl

    ld_u.wait()
    s0[...] = dot3(x_q[...].T, u[...])
    ld_t.wait()
    t1[...] = (g * 2.0 ** -0.5) * dot3(s0[...], tm[0])
    keep = pl.multiple_of(half * core, half)
    give = pl.multiple_of(half - half * core, half)
    t1_copy = send(t1.at[pl.ds(give, half)], t1_r, other)
    s0_copy = send(s0, s0_r, other)

    def member(offset):
        found = jnp.float32(0.0)
        for k in range(nlist.shape[1]):
            hit = jnp.logical_and(nlist[0, k] == me + offset, k < ncount[0])
            found = jnp.maximum(found, jnp.where(hit, 1.0, 0.0))
        return found

    m_p = member(2 - 4 * core)
    m_g = member(2 * core - 1)
    m_o = member(1 - 2 * core)
    m_b = member(4 * core - 2)

    def tile_of(a, b):
        gram = dot(a, b, NT)
        return split(gram * gram * scale)

    def apply_wide(th, tl, cat):
        wide = dot(th, cat)
        return wide[:, :2 * half] + (wide[:, 2 * half:] + dot(tl, cat[:, :2 * half]))

    ld_phi.wait()

    def own(k, carry):
        at = pl.ds(pl.multiple_of(k * 256, 256), 256)
        th, tl = tile_of(phi_q[at, :], phi_q[...])
        acc[at, :] = apply_wide(th, tl, x_cat[...])
        return carry

    lax.fori_loop(0, rows // 256, own, 0)

    def up(level, mine, received):
        s = mine + received
        ss[level - 1] = s.astype(BF16)
        if level == 4:
            return s, None, None, send(ss.at[level - 1], ss_r.at[level - 1], sib[level])
        t = (g * 2.0 ** (-0.5 * (level + 1))) * dot3(s, tm[level])
        ts[level - 1] = t.astype(BF16)
        t_copy = send(ts.at[level - 1], ts_r.at[level - 1], sib[level])
        s_copy = send(ss.at[level - 1], ss_r.at[level - 1], sib[level])
        return s, t, t_copy, s_copy

    t1_copy.wait_recv()
    s1, t2, t2_copy, s1_copy = up(1, t1[pl.ds(keep, half), :], t1_r[...])

    xo_copy.wait_recv()
    o_copy.wait_recv()
    xoh, xol = split(x_o[...])
    xo_cat = jnp.concatenate([xoh, xol], axis=1)

    def beside(k, carry):
        at = pl.ds(pl.multiple_of(k * 256, 256), 256)
        th, tl = tile_of(phi_q[at, :], phi_o[...])
        acc[at, :] += m_o * apply_wide(th, tl, xo_cat)
        return carry

    lax.fori_loop(0, rows // 256, beside, 0)

    t2_copy.wait_recv()
    s2, t3, t3_copy, s2_copy = up(2, t2, ts_r[0].astype(F32))

    fwd, back = [], []
    x_copy.wait_recv()
    xg_copy = send(x_p, x_g, other)

    def far_pair(k):
        phi_copies[k].wait_recv()
        fwd.append(send(phi_p.at[block(k)], phi_g.at[block(k)], other))
        th, tl = tile_of(phi_p[block(k), :], phi_q[...])
        bk[block(k), :] = apply_wide(th, tl, x_cat[...]).astype(BF16)
        back.append(send(bk.at[block(k)], bk_r.at[block(k)], source))
        xs = x_p[block(k), :]
        acc[...] += m_p * (dot(th, xs, TN) + dot(tl, xs, TN))

    def near_pair(k):
        fwd[k].wait_recv()
        th, tl = tile_of(phi_q[...], phi_g[block(k), :])
        xs = x_g[block(k), :]
        acc[...] += m_g * (dot(th, xs) + dot(tl, xs))

    far_pair(0)
    t3_copy.wait_recv()
    s3, t4, t4_copy, s3_copy = up(3, t3, ts_r[1].astype(F32))
    xg_copy.wait_recv()
    far_pair(1)
    near_pair(0)
    t4_copy.wait_recv()
    _, _, _, s4_copy = up(4, t4, ts_r[2].astype(F32))
    far_pair(2)
    near_pair(1)

    ld_k.wait()
    s0_copy.wait_recv()
    c0 = g * dot3(s0_r[...], km[0], NT)
    coupled = []
    for level, copy in ((1, s1_copy), (2, s2_copy), (3, s3_copy), (4, s4_copy)):
        copy.wait_recv()
        received = ss_r[level - 1]
        kh, kl = split(km[level])
        coupled.append(g * (dot(received, kh, NT) + dot(received, kl, NT)))
    e = coupled[3]
    for level in (3, 2, 1):
        e = coupled[level - 1] + (g * 2.0 ** (-0.5 * (level + 1))) * dot3(e, tm[level], NT)
    e1[...] = e
    e1_copy = send(e1, e1_r, other)
    far_pair(3)
    near_pair(2)
    e1_copy.wait_recv()
    mine, theirs = e1[...], e1_r[...]
    first = jnp.where(core == 0, mine, theirs)
    second = jnp.where(core == 0, theirs, mine)
    e0 = c0 + (g * 2.0 ** -0.5) * dot3(jnp.concatenate([first, second], axis=0), tm[0], NT)
    acc[...] += dot3(u[...], e0, NT)
    near_pair(3)
    for copy in back:
        copy.wait_recv()
    out[...] = acc[...] + m_b * bk_r[...].astype(F32)

    sent = phi_copies + [o_copy, xo_copy, x_copy, t1_copy, s0_copy, t2_copy, s1_copy, t3_copy, s2_copy, xg_copy]
    sent += fwd + back + [t4_copy, s3_copy, s4_copy, e1_copy]
    for copy in sent:
        copy.wait_send()


def shards(n, features, probes, bases, transfers, couplings, near_list, near_count):
    rows, feats = features.shape
    width = probes.shape[1]
    half = width // 2
    ranks = bases.shape[1]
    levels = transfers.shape[1]
    sends = 3 * CHUNKS + 14
    hbm = pl.BlockSpec(memory_space=pltpu.HBM)
    smem = pl.BlockSpec(memory_space=pltpu.SMEM)

    def vmem(*shape, dtype=F32):
        return pltpu.VMEM(shape, dtype)

    return pl.pallas_call(
        functools.partial(kernel, n),
        out_shape=jax.ShapeDtypeStruct((rows, width), F32),
        in_specs=[hbm] * 5 + [smem] * 2,
        out_specs=pl.BlockSpec(memory_space=pltpu.VMEM),
        scratch_shapes=[
            vmem(rows, feats, dtype=BF16), vmem(rows, feats, dtype=BF16),
            vmem(rows, feats, dtype=BF16), vmem(rows, feats, dtype=BF16),
            vmem(rows, width), vmem(rows, width),
            vmem(rows, 2 * width, dtype=BF16), vmem(rows, width, dtype=BF16),
            vmem(rows, width, dtype=BF16), vmem(rows, width, dtype=BF16),
            vmem(rows, ranks), vmem(levels, ranks, ranks), vmem(levels + 1, ranks, ranks),
            vmem(width, ranks), vmem(width, ranks), vmem(width, ranks), vmem(half, ranks),
            vmem(3, half, ranks, dtype=BF16), vmem(3, half, ranks, dtype=BF16),
            vmem(4, half, ranks, dtype=BF16), vmem(4, half, ranks, dtype=BF16),
            vmem(half, ranks), vmem(half, ranks),
            vmem(rows, width, dtype=BF16), vmem(rows, width, dtype=BF16),
            vmem(rows, width),
            pltpu.SemaphoreType.DMA((5,)),
            pltpu.SemaphoreType.DMA((sends,)),
            pltpu.SemaphoreType.DMA((sends,)),
        ],
        compiler_params=pltpu.CompilerParams(
            collective_id=0, has_side_effects=True, vmem_limit_bytes=56 * 1024 * 1024),
    )(features, probes, bases, transfers[0], couplings[0], near_list, near_count)


def solution(mesh):
    in_specs = (
        P("leaf", None),
        P("leaf", None),
        P("leaf", None),
        P("leaf", None, None, None),
        P("leaf", None, None, None),
        P("leaf", None),
        P("leaf"),
    )
    return jax.shard_map(
        functools.partial(shards, mesh.shape["leaf"]),
        mesh=mesh, in_specs=in_specs, out_specs=P("leaf", None), check_vma=False)
```

```python
import functools

import jax
import jax.numpy as jnp
from jax import lax
from jax.experimental import pallas as pl
from jax.experimental.pallas import tpu as pltpu
from jax.sharding import PartitionSpec as P

F32, BF16 = jnp.float32, jnp.bfloat16
MESH = pl.DeviceIdType.MESH
CHUNKS = 16
BLOCKS = 4
DEPTH = 3

NN = (((1,), (0,)), ((), ()))
NT = (((1,), (1,)), ((), ()))
TN = (((0,), (0,)), ((), ()))


def dot(a, b, dims=NN):
    return lax.dot_general(a, b, dims, preferred_element_type=F32)


def split(a):
    high = a.astype(BF16)
    return high, (a - high.astype(F32)).astype(BF16)


def dot3(a, b, dims=NN):
    (ah, al), (bh, bl) = split(a), split(b)
    return dot(ah, bh, dims) + (dot(ah, bl, dims) + dot(al, bh, dims))


class Move:
    def __init__(self, copy, sends=None, receives=None):
        self.copy, self.sends, self.receives = copy, sends, receives

    @staticmethod
    def run(act, when):
        if when is None:
            act()
        else:
            pl.when(when)(act)

    def start(self):
        self.run(self.copy.start, self.sends)
        return self

    def wait_send(self):
        self.run(self.copy.wait_send, self.sends)

    def wait_recv(self):
        self.run(self.copy.wait_recv, self.receives)


def kernel(n, feat, prob, base, tran, coup, nlist, ncount, out,
           phi_q, phi_p, phi_g, phi_o, x_q, x_o, x_cat, x_b, x_p, x_g, u, tm, km,
           s0, s0_r, t1, t1_r, ts, ts_r, ss, ss_r, e1, e1_r, bk, bk_r, acc,
           ld_sem, snd, rcv):
    me = lax.axis_index("leaf")
    core = lax.rem(me, 2)
    rows, feats = phi_q.shape
    ranks = u.shape[1]
    half = x_q.shape[1] // 2
    g = (3.0 / ranks) ** 0.5
    scale = 1.0 / (feats * rows)

    def flip(h):
        return (1 << h) - (2 << h) * lax.rem(me // (1 << h), 2)

    other = me + flip(0)
    source = me + 2 - 4 * core
    target = me - 2 + 4 * core
    has_source = jnp.logical_and(source >= 0, source < n)
    has_target = jnp.logical_and(target >= 0, target < n)
    sib = [other, me + flip(1), me + flip(2), me + flip(2) + flip(3), me + flip(4)]

    def load(src, dst, at):
        copy = pltpu.make_async_copy(src, dst, ld_sem.at[at])
        copy.start()
        return copy

    ld_x = load(prob, x_q, 0)
    ld_u = load(base, u, 1)
    ld_t = load(tran, tm, 2)
    ld_phi = load(feat, phi_q, 3)
    ld_k = load(coup, km, 4)

    barrier = pltpu.get_barrier_semaphore()

    def greet(p):
        pl.semaphore_signal(barrier, inc=1, device_id=(p,), device_id_type=MESH)

    for p in (other, sib[2], sib[3], sib[4]):
        greet(p)
    pl.when(has_source)(lambda: greet(source))
    pl.when(has_target)(lambda: greet(target))
    pl.semaphore_wait(barrier, 4 + has_source.astype(jnp.int32) + has_target.astype(jnp.int32))

    count, sent = [0], []

    def move(src, dst, to, sends=None, receives=None):
        at = count[0]
        count[0] += 1
        return Move(pltpu.make_async_remote_copy(
            src_ref=src, dst_ref=dst, send_sem=snd.at[at], recv_sem=rcv.at[at],
            device_id=(to,), device_id_type=MESH), sends, receives)

    def send(*args):
        sent.append(move(*args).start())
        return sent[-1]

    def ahead(src, dst):
        return move(src, dst, target, has_target, has_source)

    def part(k, parts):
        return pl.ds(k * (rows // parts), rows // parts)

    phi_moves = [ahead(feat.at[part(k, CHUNKS)], phi_p.at[part(k, CHUNKS)]) for k in range(CHUNKS)]
    x_moves = [ahead(x_b.at[part(k, 2)], x_p.at[part(k, 2)]) for k in range(2)]
    waiting = phi_moves[:5] + x_moves + phi_moves[5:]
    flying = []

    def pump(times=1):
        for _ in range(times):
            if waiting:
                if len(flying) == DEPTH:
                    flying.pop(0).wait_send()
                flying.append(waiting.pop(0).start())

    pump(DEPTH)
    o_moves = [send(feat.at[part(k, 2)], phi_o.at[part(k, 2)], other) for k in range(2)]
    xo_move = send(prob, x_o, other)

    @pl.when(jnp.logical_not(has_source))
    def _():
        phi_p[...] = jnp.zeros_like(phi_p)
        x_p[...] = jnp.zeros_like(x_p)

    @pl.when(jnp.logical_not(has_target))
    def _():
        bk_r[...] = jnp.zeros_like(bk_r)

    ld_x.wait()
    xh, xl = split(x_q[...])
    x_b[...] = xh
    x_cat[:, :2 * half] = xh
    x_cat[:, 2 * half:] = xl

    ld_u.wait()
    s0[...] = dot3(x_q[...].T, u[...])
    ld_t.wait()
    t1[...] = (g * 2.0 ** -0.5) * dot3(s0[...], tm[0])
    keep = pl.multiple_of(half * core, half)
    give = pl.multiple_of(half - half * core, half)
    t1_move = send(t1.at[pl.ds(give, half)], t1_r, other)
    s0_move = send(s0, s0_r, other)
    pump()

    def member(offset):
        found = jnp.float32(0.0)
        for k in range(nlist.shape[1]):
            hit = jnp.logical_and(nlist[0, k] == me + offset, k < ncount[0])
            found = jnp.maximum(found, jnp.where(hit, 1.0, 0.0))
        return found

    m_p = member(2 - 4 * core)
    m_g = member(2 * core - 1)
    m_o = member(1 - 2 * core)
    m_b = member(4 * core - 2)

    def tile_of(a, b):
        gram = dot(a, b, NT)
        return split(gram * gram * scale)

    def apply_wide(th, tl, cat):
        wide = dot(th, cat)
        return wide[:, :2 * half] + (wide[:, 2 * half:] + dot(tl, cat[:, :2 * half]))

    def own(k):
        th, tl = tile_of(phi_q[part(k, 2), :], phi_q[...])
        acc[part(k, 2), :] = apply_wide(th, tl, x_cat[...])

    def beside(k):
        if k == 0:
            xo_move.wait_recv()
        o_moves[k].wait_recv()
        th, tl = tile_of(phi_q[...], phi_o[part(k, 2), :])
        xoh, xol = split(x_o[part(k, 2), :])
        acc[...] += m_o * apply_wide(th, tl, jnp.concatenate([xoh, xol], axis=1))

    def up(level, mine, received):
        s = mine + received
        ss[level - 1] = s.astype(BF16)
        if level == 4:
            return None, None, send(ss.at[level - 1], ss_r.at[level - 1], sib[level])
        t = (g * 2.0 ** (-0.5 * (level + 1))) * dot3(s, tm[level])
        ts[level - 1] = t.astype(BF16)
        t_move = send(ts.at[level - 1], ts_r.at[level - 1], sib[level])
        s_move = send(ss.at[level - 1], ss_r.at[level - 1], sib[level])
        return t, t_move, s_move

    fwd, back = [], []

    def far_pair(k):
        if k == 0:
            for m in x_moves:
                m.wait_recv()
            fwd.append(send(x_p, x_g, other))
        for m in phi_moves[k * CHUNKS // BLOCKS:(k + 1) * CHUNKS // BLOCKS]:
            m.wait_recv()
        at = part(k, BLOCKS)
        fwd.append(send(phi_p.at[at], phi_g.at[at], other))
        th, tl = tile_of(phi_p[at, :], phi_q[...])
        bk[at, :] = apply_wide(th, tl, x_cat[...]).astype(BF16)
        back.append(send(bk.at[at], bk_r.at[at], source, has_source, has_target))
        xs = x_p[at, :]
        acc[...] += m_p * (dot(th, xs, TN) + dot(tl, xs, TN))

    def near_pair(k):
        if k == 0:
            fwd[0].wait_recv()
        fwd[k + 1].wait_recv()
        at = part(k, BLOCKS)
        th, tl = tile_of(phi_q[...], phi_g[at, :])
        xs = x_g[at, :]
        acc[...] += m_g * (dot(th, xs) + dot(tl, xs))

    coupled = [None] * 5

    def couple(level, move):
        move.wait_recv()
        if level == 0:
            coupled[0] = g * dot3(s0_r[...], km[0], NT)
        else:
            received = ss_r[level - 1]
            kh, kl = split(km[level])
            coupled[level] = g * (dot(received, kh, NT) + dot(received, kl, NT))

    ld_phi.wait()
    own(0)
    pump()
    t1_move.wait_recv()
    t2, t2_move, s1_move = up(1, t1[pl.ds(keep, half), :], t1_r[...])
    pump()
    own(1)
    pump()
    beside(0)
    pump()
    t2_move.wait_recv()
    t3, t3_move, s2_move = up(2, t2, ts_r[0].astype(F32))
    pump()
    beside(1)
    pump()
    ld_k.wait()
    couple(0, s0_move)
    pump()
    t3_move.wait_recv()
    t4, t4_move, s3_move = up(3, t3, ts_r[1].astype(F32))
    pump()
    far_pair(0)
    pump()
    couple(1, s1_move)
    pump()
    t4_move.wait_recv()
    _, _, s4_move = up(4, t4, ts_r[2].astype(F32))
    pump()
    far_pair(1)
    pump()
    near_pair(0)
    pump()
    couple(2, s2_move)
    couple(3, s3_move)
    pump(2)
    far_pair(2)
    pump(len(waiting))
    couple(4, s4_move)
    e = coupled[4]
    for level in (3, 2, 1):
        e = coupled[level] + (g * 2.0 ** (-0.5 * (level + 1))) * dot3(e, tm[level], NT)
    e1[...] = e
    e1_move = send(e1, e1_r, other)
    near_pair(1)
    far_pair(3)
    near_pair(2)
    e1_move.wait_recv()
    mine, theirs = e1[...], e1_r[...]
    first = jnp.where(core == 0, mine, theirs)
    second = jnp.where(core == 0, theirs, mine)
    e0 = coupled[0] + (g * 2.0 ** -0.5) * dot3(jnp.concatenate([first, second], axis=0), tm[0], NT)
    acc[...] += dot3(u[...], e0, NT)
    near_pair(3)
    for m in back:
        m.wait_recv()
    out[...] = acc[...] + m_b * bk_r[...].astype(F32)
    for m in flying + sent:
        m.wait_send()


def shards(n, features, probes, bases, transfers, couplings, near_list, near_count):
    rows, feats = features.shape
    width = probes.shape[1]
    half = width // 2
    ranks = bases.shape[1]
    levels = transfers.shape[1]
    sends = CHUNKS + 2 * BLOCKS + 17
    hbm = pl.BlockSpec(memory_space=pltpu.HBM)
    smem = pl.BlockSpec(memory_space=pltpu.SMEM)

    def vmem(*shape, dtype=F32):
        return pltpu.VMEM(shape, dtype)

    return pl.pallas_call(
        functools.partial(kernel, n),
        out_shape=jax.ShapeDtypeStruct((rows, width), F32),
        in_specs=[hbm] * 5 + [smem] * 2,
        out_specs=pl.BlockSpec(memory_space=pltpu.VMEM),
        scratch_shapes=[
            vmem(rows, feats, dtype=BF16), vmem(rows, feats, dtype=BF16),
            vmem(rows, feats, dtype=BF16), vmem(rows, feats, dtype=BF16),
            vmem(rows, width), vmem(rows, width),
            vmem(rows, 2 * width, dtype=BF16), vmem(rows, width, dtype=BF16),
            vmem(rows, width, dtype=BF16), vmem(rows, width, dtype=BF16),
            vmem(rows, ranks), vmem(levels, ranks, ranks), vmem(levels + 1, ranks, ranks),
            vmem(width, ranks), vmem(width, ranks), vmem(width, ranks), vmem(half, ranks),
            vmem(3, half, ranks, dtype=BF16), vmem(3, half, ranks, dtype=BF16),
            vmem(4, half, ranks, dtype=BF16), vmem(4, half, ranks, dtype=BF16),
            vmem(half, ranks), vmem(half, ranks),
            vmem(rows, width, dtype=BF16), vmem(rows, width, dtype=BF16),
            vmem(rows, width),
            pltpu.SemaphoreType.DMA((5,)),
            pltpu.SemaphoreType.DMA((sends,)),
            pltpu.SemaphoreType.DMA((sends,)),
        ],
        compiler_params=pltpu.CompilerParams(
            collective_id=0, has_side_effects=True, vmem_limit_bytes=56 * 1024 * 1024),
    )(features, probes, bases, transfers[0], couplings[0], near_list, near_count)


def solution(mesh):
    in_specs = (
        P("leaf", None),
        P("leaf", None),
        P("leaf", None),
        P("leaf", None, None, None),
        P("leaf", None, None, None),
        P("leaf", None),
        P("leaf"),
    )
    return jax.shard_map(
        functools.partial(shards, mesh.shape["leaf"]),
        mesh=mesh, in_specs=in_specs, out_specs=P("leaf", None), check_vma=False)
```

```python
import functools

import jax
import jax.numpy as jnp
from jax import lax
from jax.experimental import pallas as pl
from jax.experimental.pallas import tpu as pltpu
from jax.sharding import PartitionSpec as P

F32, BF16 = jnp.float32, jnp.bfloat16
MESH = pl.DeviceIdType.MESH
CHUNKS = 16
BLOCKS = ((0, 256), (256, 128), (384, 128))
BURSTS = (5, 6, 7)

NN = (((1,), (0,)), ((), ()))
NT = (((1,), (1,)), ((), ()))
TN = (((0,), (0,)), ((), ()))


def dot(a, b, dims=NN):
    return lax.dot_general(a, b, dims, preferred_element_type=F32)


def split(a):
    high = a.astype(BF16)
    return high, (a - high.astype(F32)).astype(BF16)


def dot3(a, b, dims=NN):
    (ah, al), (bh, bl) = split(a), split(b)
    return dot(ah, bh, dims) + (dot(ah, bl, dims) + dot(al, bh, dims))


class Move:
    def __init__(self, copy, sends=None, receives=None):
        self.copy, self.sends, self.receives = copy, sends, receives

    @staticmethod
    def run(act, when):
        if when is None:
            act()
        else:
            pl.when(when)(act)

    def start(self):
        self.run(self.copy.start, self.sends)
        return self

    def wait_send(self):
        self.run(self.copy.wait_send, self.sends)

    def wait_recv(self):
        self.run(self.copy.wait_recv, self.receives)


def kernel(n, feat, prob, base, tran, coup, nlist_hbm, ncount_hbm, out,
           phi_q, phi_p, phi_g, phi_o, x_q, x_o, x_cat, x_b, x_p, x_g, u, tm, km,
           s0, s0_r, t1, t1_r, t2, t2_r, v3, v3_r, t4, ss, ss_r, e1, e1_r, bk, bk_r, acc,
           nlist, ncount, ld_sem, snd, rcv):
    me = lax.axis_index("leaf")
    core = lax.rem(me, 2)
    rows, feats = phi_q.shape
    ranks = u.shape[1]
    half = x_q.shape[1] // 2
    g = (3.0 / ranks) ** 0.5
    scale = 1.0 / (feats * rows)

    def flip(h):
        return (1 << h) - (2 << h) * lax.rem(me // (1 << h), 2)

    other = me + flip(0)
    source = me + 2 - 4 * core
    target = me - 2 + 4 * core
    has_source = jnp.logical_and(source >= 0, source < n)
    has_target = jnp.logical_and(target >= 0, target < n)
    next_chip, cross, cross_next = me + flip(1), me + flip(2), me + flip(1) + flip(2)
    level3 = me + flip(2) + flip(3)
    level4, level4_far = me + flip(4), me + flip(2) + flip(3) + flip(4)
    early = lax.rem(me // 2, 8) < 4
    late = jnp.logical_not(early)

    barrier = pltpu.get_barrier_semaphore()

    def greet(p):
        pl.semaphore_signal(barrier, inc=1, device_id=(p,), device_id_type=MESH)

    fixed = (other, cross_next, level4_far, level3, cross, level4)
    pl.when(has_target)(lambda: greet(target))
    pl.when(has_source)(lambda: greet(source))
    for p in fixed:
        greet(p)

    def load(src, dst, at):
        copy = pltpu.make_async_copy(src, dst, ld_sem.at[at])
        copy.start()
        return copy

    ld_x = load(prob, x_q, 0)
    ld_u = load(base, u, 1)
    ld_t = load(tran, tm, 2)
    ld_phi = load(feat, phi_q, 3)
    ld_k = load(coup, km, 4)
    ld_list = load(nlist_hbm, nlist, 5)
    ld_count = load(ncount_hbm, ncount, 6)

    def member(offset):
        found = jnp.float32(0.0)
        for k in range(nlist.shape[1]):
            hit = jnp.logical_and(nlist[0, k] == me + offset, k < ncount[0])
            found = jnp.maximum(found, jnp.where(hit, 1.0, 0.0))
        return found

    def tile_of(a, b):
        gram = dot(a, b, NT)
        return split(gram * gram * scale)

    def apply_wide(th, tl, cat):
        wide = dot(th, cat)
        return wide[:, :2 * half] + (wide[:, 2 * half:] + dot(tl, cat[:, :2 * half]))

    def split_probes():
        ld_x.wait()
        xh, xl = split(x_q[...])
        x_b[...] = xh
        x_cat[:, :2 * half] = xh
        x_cat[:, 2 * half:] = xl

    def own():
        def step(k, carry):
            at = pl.ds(pl.multiple_of(k * 256, 256), 256)
            th, tl = tile_of(phi_q[at, :], phi_q[...])
            acc[at, :] += apply_wide(th, tl, x_cat[...])
            return carry

        lax.fori_loop(0, rows // 256, step, 0)

    acc[...] = jnp.zeros_like(acc)

    @pl.when(early)
    def _():
        split_probes()
        for ld in (ld_u, ld_t, ld_phi, ld_k):
            ld.wait()
        own()

    pl.semaphore_wait(barrier, len(fixed) + has_source.astype(jnp.int32) + has_target.astype(jnp.int32))

    count, sent = [0], []

    def move(src, dst, to, sends=None, receives=None):
        at = count[0]
        count[0] += 1
        return Move(pltpu.make_async_remote_copy(
            src_ref=src, dst_ref=dst, send_sem=snd.at[at], recv_sem=rcv.at[at],
            device_id=(to,), device_id_type=MESH), sends, receives)

    def send(*args):
        sent.append(move(*args).start())
        return sent[-1]

    def ahead(src, dst):
        return move(src, dst, target, has_target, has_source)

    def part(k, parts):
        return pl.ds(k * (rows // parts), rows // parts)

    phi_moves = [ahead(feat.at[part(k, CHUNKS)], phi_p.at[part(k, CHUNKS)]) for k in range(CHUNKS)]
    x_moves = [ahead(x_b.at[part(k, 2)], x_p.at[part(k, 2)]) for k in range(2)]
    waiting = phi_moves[:6] + x_moves + phi_moves[6:]

    def burst(times):
        for _ in range(times):
            waiting.pop(0).start()

    burst(BURSTS[0])
    o_moves = [send(feat.at[part(k, 2)], phi_o.at[part(k, 2)], other) for k in range(2)]
    xo_move = send(prob, x_o, other)

    @pl.when(jnp.logical_not(has_source))
    def _():
        phi_p[...] = jnp.zeros_like(phi_p)
        x_p[...] = jnp.zeros_like(x_p)

    @pl.when(jnp.logical_not(has_target))
    def _():
        bk_r[...] = jnp.zeros_like(bk_r)

    pl.when(late)(split_probes)

    pl.when(late)(ld_u.wait)
    s0[...] = dot3(x_q[...].T, u[...])
    pl.when(late)(ld_t.wait)
    t1[...] = (g * 2.0 ** -0.5) * dot3(s0[...], tm[0])
    keep = pl.multiple_of(half * core, half)
    give = pl.multiple_of(half - half * core, half)
    t1_move = send(t1.at[pl.ds(give, half)], t1_r, other)
    s0_move = send(s0, s0_r, other)

    ld_list.wait()
    ld_count.wait()
    m_p = member(2 - 4 * core)
    m_g = member(2 * core - 1)
    m_o = member(1 - 2 * core)
    m_b = member(4 * core - 2)

    def beside(k):
        if k == 0:
            xo_move.wait_recv()
        o_moves[k].wait_recv()
        th, tl = tile_of(phi_q[...], phi_o[part(k, 2), :])
        xoh, xol = split(x_o[part(k, 2), :])
        acc[...] += m_o * apply_wide(th, tl, jnp.concatenate([xoh, xol], axis=1))

    fwd, back = [], []

    def far_pair(k):
        start, length = BLOCKS[k]
        at = pl.ds(start, length)
        if k == 0:
            for m in x_moves:
                m.wait_recv()
            fwd.append(send(x_p, x_g, other))
        for m in phi_moves[start * CHUNKS // rows:(start + length) * CHUNKS // rows]:
            m.wait_recv()
        fwd.append(send(phi_p.at[at], phi_g.at[at], other))
        th, tl = tile_of(phi_p[at, :], phi_q[...])
        bk[at, :] = apply_wide(th, tl, x_cat[...]).astype(BF16)
        back.append(send(bk.at[at], bk_r.at[at], source, has_source, has_target))
        xs = x_p[at, :]
        acc[...] += m_p * (dot(th, xs, TN) + dot(tl, xs, TN))

    def near_pair(k):
        start, length = BLOCKS[k]
        at = pl.ds(start, length)
        if k == 0:
            fwd[0].wait_recv()
        fwd[k + 1].wait_recv()
        th, tl = tile_of(phi_q[...], phi_g[at, :])
        xs = x_g[at, :]
        acc[...] += m_g * (dot(th, xs) + dot(tl, xs))

    def factor(level):
        return g * 2.0 ** (-0.5 * level)

    t1_move.wait_recv()
    s1 = t1[pl.ds(keep, half), :] + t1_r[...]
    mine2 = factor(2) * dot3(s1, tm[1])
    t2[...] = mine2.astype(BF16)
    t2_move = send(t2, t2_r, next_chip)
    mine3 = factor(3) * dot3(mine2, tm[2])
    v3[...] = mine3.astype(BF16)
    v3_moves = [send(v3, v3_r.at[1], cross_next), send(v3, v3_r.at[0], cross)]
    ss[0] = s1.astype(BF16)
    s1_move = send(ss.at[0], ss_r.at[0], next_chip)
    burst(BURSTS[1])
    pl.when(late)(ld_phi.wait)
    beside(0)
    beside(1)

    t2_move.wait_recv()
    from2 = t2_r[...]
    ss[1] = (mine2 + from2.astype(F32)).astype(BF16)
    s2_move = send(ss.at[1], ss_r.at[1], cross)
    t2h, t2l = split(tm[2])
    mine3 = mine3 + factor(3) * (dot(from2, t2h) + dot(from2, t2l))
    pl.when(late)(ld_k.wait)
    s0_move.wait_recv()
    e0 = g * dot3(s0_r[...], km[0], NT)
    for m in v3_moves:
        m.wait_recv()
    s3 = mine3 + (v3_r[0].astype(F32) + v3_r[1].astype(F32))
    t4[...] = (factor(4) * dot3(s3, tm[3])).astype(BF16)
    t4_moves = [send(t4, ss_r.at[4], level4_far), send(t4, ss_r.at[3], level4)]
    ss[2] = s3.astype(BF16)
    s3_move = send(ss.at[2], ss_r.at[2], level3)
    burst(BURSTS[2])

    def couple(level, m):
        m.wait_recv()
        received = ss_r[level - 1]
        kh, kl = split(km[level])
        return g * (dot(received, kh, NT) + dot(received, kl, NT))

    coupled1 = couple(1, s1_move)
    far_pair(0)
    near_pair(0)
    coupled2 = couple(2, s2_move)
    far_pair(1)
    for m in t4_moves:
        m.wait_recv()
    e = g * dot3(ss_r[3].astype(F32) + ss_r[4].astype(F32), km[4], NT)
    e = couple(3, s3_move) + factor(4) * dot3(e, tm[3], NT)
    e = coupled2 + factor(3) * dot3(e, tm[2], NT)
    e1[...] = coupled1 + factor(2) * dot3(e, tm[1], NT)
    e1_move = send(e1, e1_r, other)
    near_pair(1)
    far_pair(2)
    e1_move.wait_recv()
    mine, theirs = e1[...], e1_r[...]
    first = jnp.where(core == 0, mine, theirs)
    second = jnp.where(core == 0, theirs, mine)
    e0 = e0 + factor(1) * dot3(jnp.concatenate([first, second], axis=0), tm[0], NT)
    acc[...] += dot3(u[...], e0, NT)
    near_pair(2)
    pl.when(late)(own)
    for m in back:
        m.wait_recv()
    out[...] = acc[...] + m_b * bk_r[...].astype(F32)
    for m in phi_moves + x_moves + sent:
        m.wait_send()


def shards(n, features, probes, bases, transfers, couplings, near_list, near_count):
    rows, feats = features.shape
    width = probes.shape[1]
    half = width // 2
    ranks = bases.shape[1]
    levels = transfers.shape[1]
    sends = CHUNKS + 2 * len(BLOCKS) + 17
    hbm = pl.BlockSpec(memory_space=pltpu.HBM)

    def vmem(*shape, dtype=F32):
        return pltpu.VMEM(shape, dtype)

    return pl.pallas_call(
        functools.partial(kernel, n),
        out_shape=jax.ShapeDtypeStruct((rows, width), F32),
        in_specs=[hbm] * 7,
        out_specs=pl.BlockSpec(memory_space=pltpu.VMEM),
        scratch_shapes=[
            vmem(rows, feats, dtype=BF16), vmem(rows, feats, dtype=BF16),
            vmem(rows, feats, dtype=BF16), vmem(rows, feats, dtype=BF16),
            vmem(rows, width), vmem(rows, width),
            vmem(rows, 2 * width, dtype=BF16), vmem(rows, width, dtype=BF16),
            vmem(rows, width, dtype=BF16), vmem(rows, width, dtype=BF16),
            vmem(rows, ranks), vmem(levels, ranks, ranks), vmem(levels + 1, ranks, ranks),
            vmem(width, ranks), vmem(width, ranks), vmem(width, ranks), vmem(half, ranks),
            vmem(half, ranks, dtype=BF16), vmem(half, ranks, dtype=BF16),
            vmem(half, ranks, dtype=BF16), vmem(2, half, ranks, dtype=BF16),
            vmem(half, ranks, dtype=BF16), vmem(3, half, ranks, dtype=BF16),
            vmem(5, half, ranks, dtype=BF16), vmem(half, ranks), vmem(half, ranks),
            vmem(rows, width, dtype=BF16), vmem(rows, width, dtype=BF16),
            vmem(rows, width),
            pltpu.SMEM((1, 4), jnp.int32), pltpu.SMEM((1,), jnp.int32),
            pltpu.SemaphoreType.DMA((7,)),
            pltpu.SemaphoreType.DMA((sends,)),
            pltpu.SemaphoreType.DMA((sends,)),
        ],
        compiler_params=pltpu.CompilerParams(
            collective_id=0, has_side_effects=True, vmem_limit_bytes=56 * 1024 * 1024),
    )(features, probes, bases, transfers[0], couplings[0], near_list, near_count)


def solution(mesh):
    in_specs = (
        P("leaf", None),
        P("leaf", None),
        P("leaf", None),
        P("leaf", None, None, None),
        P("leaf", None, None, None),
        P("leaf", None),
        P("leaf"),
    )
    return jax.shard_map(
        functools.partial(shards, mesh.shape["leaf"]),
        mesh=mesh, in_specs=in_specs, out_specs=P("leaf", None), check_vma=False)
```

```python
import functools

import jax
import jax.numpy as jnp
from jax import lax
from jax.experimental import pallas as pl
from jax.experimental.pallas import tpu as pltpu
from jax.sharding import PartitionSpec as P

F32, BF16 = jnp.float32, jnp.bfloat16
MESH = pl.DeviceIdType.MESH
CHUNKS = 16
BLOCKS = ((0, 256), (256, 128), (384, 128))
BURSTS = (5, 6, 7)
FIRST_BURSTS = (18, 0, 0)

NN = (((1,), (0,)), ((), ()))
NT = (((1,), (1,)), ((), ()))
TN = (((0,), (0,)), ((), ()))


def dot(a, b, dims=NN):
    return lax.dot_general(a, b, dims, preferred_element_type=F32)


def split(a):
    high = a.astype(BF16)
    return high, (a - high.astype(F32)).astype(BF16)


def dot3(a, b, dims=NN):
    (ah, al), (bh, bl) = split(a), split(b)
    return dot(ah, bh, dims) + (dot(ah, bl, dims) + dot(al, bh, dims))


class Move:
    def __init__(self, copy, sends=None, receives=None):
        self.copy, self.sends, self.receives = copy, sends, receives

    @staticmethod
    def run(act, when):
        if when is None:
            act()
        else:
            pl.when(when)(act)

    def start(self, when=None):
        self.run(self.copy.start, self.sends if when is None else jnp.logical_and(self.sends, when))
        return self

    def wait_send(self):
        self.run(self.copy.wait_send, self.sends)

    def wait_recv(self):
        self.run(self.copy.wait_recv, self.receives)


def kernel(n, feat, prob, base, tran, coup, nlist_hbm, ncount_hbm, out,
           phi_q, phi_p, phi_g, phi_o, x_q, x_o, x_cat, x_b, x_p, x_g, u, tm, km,
           s0, s0_r, t1, t1_r, t2, t2_r, v3, v3_r, t4, ss, ss_r, e1, e1_r, bk, bk_r, acc,
           nlist, ncount, ld_sem, snd, rcv):
    me = lax.axis_index("leaf")
    core = lax.rem(me, 2)
    rows, feats = phi_q.shape
    ranks = u.shape[1]
    half = x_q.shape[1] // 2
    g = (3.0 / ranks) ** 0.5
    scale = 1.0 / (feats * rows)

    def flip(h):
        return (1 << h) - (2 << h) * lax.rem(me // (1 << h), 2)

    other = me + flip(0)
    source = me + 2 - 4 * core
    target = me - 2 + 4 * core
    has_source = jnp.logical_and(source >= 0, source < n)
    has_target = jnp.logical_and(target >= 0, target < n)
    next_chip, cross, cross_next = me + flip(1), me + flip(2), me + flip(1) + flip(2)
    level3 = me + flip(2) + flip(3)
    level4, level4_far = me + flip(4), me + flip(2) + flip(3) + flip(4)
    early = lax.rem(me // 2, 8) < 4
    late = jnp.logical_not(early)
    hurried = lax.rem(me, 16) == 0
    row_end = lax.rem(me // 2, 8) == 7

    barrier = pltpu.get_barrier_semaphore()

    def greet(p):
        pl.semaphore_signal(barrier, inc=1, device_id=(p,), device_id_type=MESH)

    fixed = (other, cross_next, level4_far, level3, cross, level4)
    pl.when(has_target)(lambda: greet(target))
    pl.when(has_source)(lambda: greet(source))
    for p in fixed:
        greet(p)

    def load(src, dst, at):
        copy = pltpu.make_async_copy(src, dst, ld_sem.at[at])
        copy.start()
        return copy

    ld_x = load(prob, x_q, 0)
    ld_u = load(base, u, 1)
    ld_t = load(tran, tm, 2)
    ld_phi = load(feat, phi_q, 3)
    ld_k = load(coup, km, 4)
    ld_list = load(nlist_hbm, nlist, 5)
    ld_count = load(ncount_hbm, ncount, 6)

    def member(offset):
        found = jnp.float32(0.0)
        for k in range(nlist.shape[1]):
            hit = jnp.logical_and(nlist[0, k] == me + offset, k < ncount[0])
            found = jnp.maximum(found, jnp.where(hit, 1.0, 0.0))
        return found

    def tile_of(a, b):
        gram = dot(a, b, NT)
        return split(gram * gram * scale)

    def apply_wide(th, tl, cat):
        wide = dot(th, cat)
        return wide[:, :2 * half] + (wide[:, 2 * half:] + dot(tl, cat[:, :2 * half]))

    def split_probes():
        ld_x.wait()
        xh, xl = split(x_q[...])
        x_b[...] = xh
        x_cat[:, :2 * half] = xh
        x_cat[:, 2 * half:] = xl

    def own():
        def step(k, carry):
            at = pl.ds(pl.multiple_of(k * 256, 256), 256)
            th, tl = tile_of(phi_q[at, :], phi_q[...])
            acc[at, :] += apply_wide(th, tl, x_cat[...])
            return carry

        lax.fori_loop(0, rows // 256, step, 0)

    acc[...] = jnp.zeros_like(acc)

    @pl.when(early)
    def _():
        split_probes()
        for ld in (ld_u, ld_t, ld_phi, ld_k):
            ld.wait()
        own()

    pl.semaphore_wait(barrier, len(fixed) + has_source.astype(jnp.int32) + has_target.astype(jnp.int32))

    count, sent = [0], []

    def move(src, dst, to, sends=None, receives=None):
        at = count[0]
        count[0] += 1
        return Move(pltpu.make_async_remote_copy(
            src_ref=src, dst_ref=dst, send_sem=snd.at[at], recv_sem=rcv.at[at],
            device_id=(to,), device_id_type=MESH), sends, receives)

    def send(*args):
        sent.append(move(*args).start())
        return sent[-1]

    def ahead(src, dst):
        return move(src, dst, target, has_target, has_source)

    def part(k, parts):
        return pl.ds(k * (rows // parts), rows // parts)

    phi_moves = [ahead(feat.at[part(k, CHUNKS)], phi_p.at[part(k, CHUNKS)]) for k in range(CHUNKS)]
    x_moves = [ahead(x_b.at[part(k, 2)], x_p.at[part(k, 2)]) for k in range(2)]
    waiting = phi_moves[:6] + x_moves + phi_moves[6:]

    def burst(stage):
        for k, m in enumerate(waiting):
            plain = sum(BURSTS[:stage]) <= k < sum(BURSTS[:stage + 1])
            sooner = sum(FIRST_BURSTS[:stage]) <= k < sum(FIRST_BURSTS[:stage + 1])
            if plain and sooner:
                m.start()
            elif plain:
                m.start(jnp.logical_not(hurried))
            elif sooner:
                m.start(hurried)

    burst(0)
    o_moves = [send(feat.at[part(k, 2)], phi_o.at[part(k, 2)], other) for k in range(2)]
    xo_move = send(prob, x_o, other)

    @pl.when(jnp.logical_not(has_source))
    def _():
        phi_p[...] = jnp.zeros_like(phi_p)
        x_p[...] = jnp.zeros_like(x_p)

    @pl.when(jnp.logical_not(has_target))
    def _():
        bk_r[...] = jnp.zeros_like(bk_r)

    pl.when(late)(split_probes)

    pl.when(late)(ld_u.wait)
    s0[...] = dot3(x_q[...].T, u[...])
    pl.when(late)(ld_t.wait)
    t1[...] = (g * 2.0 ** -0.5) * dot3(s0[...], tm[0])
    keep = pl.multiple_of(half * core, half)
    give = pl.multiple_of(half - half * core, half)
    t1_move = send(t1.at[pl.ds(give, half)], t1_r, other)
    s0_move = send(s0, s0_r, other)

    ld_list.wait()
    ld_count.wait()
    m_p = member(2 - 4 * core)
    m_g = member(2 * core - 1)
    m_o = member(1 - 2 * core)
    m_b = member(4 * core - 2)

    def beside(k):
        if k == 0:
            xo_move.wait_recv()
        o_moves[k].wait_recv()
        th, tl = tile_of(phi_q[...], phi_o[part(k, 2), :])
        xoh, xol = split(x_o[part(k, 2), :])
        acc[...] += m_o * apply_wide(th, tl, jnp.concatenate([xoh, xol], axis=1))

    spans = [pl.ds(start, length) for start, length in BLOCKS]
    xg_move = move(x_p, x_g, other)
    fwd = [move(phi_p.at[at], phi_g.at[at], other) for at in spans]
    back = [move(bk.at[at], bk_r.at[at], source, has_source, has_target) for at in spans]

    def far_pair(k):
        start, length = BLOCKS[k]
        at = spans[k]
        if k == 0:
            for m in x_moves:
                m.wait_recv()
            xg_move.start()
        for m in phi_moves[start * CHUNKS // rows:(start + length) * CHUNKS // rows]:
            m.wait_recv()
        fwd[k].start()
        th, tl = tile_of(phi_p[at, :], phi_q[...])
        bk[at, :] = apply_wide(th, tl, x_cat[...]).astype(BF16)
        back[k].start()
        xs = x_p[at, :]
        acc[...] += m_p * (dot(th, xs, TN) + dot(tl, xs, TN))

    def near_pair(k):
        at = spans[k]
        if k == 0:
            xg_move.wait_recv()
        fwd[k].wait_recv()
        th, tl = tile_of(phi_q[...], phi_g[at, :])
        xs = x_g[at, :]
        acc[...] += m_g * (dot(th, xs) + dot(tl, xs))

    def factor(level):
        return g * 2.0 ** (-0.5 * level)

    t1_move.wait_recv()
    s1 = t1[pl.ds(keep, half), :] + t1_r[...]
    mine2 = factor(2) * dot3(s1, tm[1])
    t2[...] = mine2.astype(BF16)
    t2_move = send(t2, t2_r, next_chip)
    mine3 = factor(3) * dot3(mine2, tm[2])
    v3[...] = mine3.astype(BF16)
    v3_moves = [send(v3, v3_r.at[1], cross_next), send(v3, v3_r.at[0], cross)]
    ss[0] = s1.astype(BF16)
    s1_move = send(ss.at[0], ss_r.at[0], next_chip)
    burst(1)
    pl.when(late)(ld_phi.wait)
    beside(0)
    beside(1)

    t2_move.wait_recv()
    from2 = t2_r[...]
    ss[1] = (mine2 + from2.astype(F32)).astype(BF16)
    s2_move = send(ss.at[1], ss_r.at[1], cross)
    t2h, t2l = split(tm[2])
    mine3 = mine3 + factor(3) * (dot(from2, t2h) + dot(from2, t2l))
    pl.when(late)(ld_k.wait)
    s0_move.wait_recv()
    e0 = g * dot3(s0_r[...], km[0], NT)
    for m in v3_moves:
        m.wait_recv()
    s3 = mine3 + (v3_r[0].astype(F32) + v3_r[1].astype(F32))
    t4[...] = (factor(4) * dot3(s3, tm[3])).astype(BF16)
    t4_moves = [send(t4, ss_r.at[4], level4_far), send(t4, ss_r.at[3], level4)]
    ss[2] = s3.astype(BF16)
    s3_move = send(ss.at[2], ss_r.at[2], level3)
    burst(2)

    def couple(level, m):
        m.wait_recv()
        received = ss_r[level - 1]
        kh, kl = split(km[level])
        return g * (dot(received, kh, NT) + dot(received, kl, NT))

    coupled1 = couple(1, s1_move)
    far_pair(0)
    near_pair(0)
    coupled2 = couple(2, s2_move)
    far_pair(1)
    pl.when(row_end)(lambda: far_pair(2))
    for m in t4_moves:
        m.wait_recv()
    e = g * dot3(ss_r[3].astype(F32) + ss_r[4].astype(F32), km[4], NT)
    e = couple(3, s3_move) + factor(4) * dot3(e, tm[3], NT)
    e = coupled2 + factor(3) * dot3(e, tm[2], NT)
    e1[...] = coupled1 + factor(2) * dot3(e, tm[1], NT)
    e1_move = send(e1, e1_r, other)
    near_pair(1)
    pl.when(jnp.logical_not(row_end))(lambda: far_pair(2))
    e1_move.wait_recv()
    mine, theirs = e1[...], e1_r[...]
    first = jnp.where(core == 0, mine, theirs)
    second = jnp.where(core == 0, theirs, mine)
    e0 = e0 + factor(1) * dot3(jnp.concatenate([first, second], axis=0), tm[0], NT)
    acc[...] += dot3(u[...], e0, NT)
    near_pair(2)
    pl.when(late)(own)
    for m in back:
        m.wait_recv()
    out[...] = acc[...] + m_b * bk_r[...].astype(F32)
    for m in phi_moves + x_moves + fwd + back + [xg_move] + sent:
        m.wait_send()


def shards(n, features, probes, bases, transfers, couplings, near_list, near_count):
    rows, feats = features.shape
    width = probes.shape[1]
    half = width // 2
    ranks = bases.shape[1]
    levels = transfers.shape[1]
    sends = CHUNKS + 2 * len(BLOCKS) + 17
    hbm = pl.BlockSpec(memory_space=pltpu.HBM)

    def vmem(*shape, dtype=F32):
        return pltpu.VMEM(shape, dtype)

    return pl.pallas_call(
        functools.partial(kernel, n),
        out_shape=jax.ShapeDtypeStruct((rows, width), F32),
        in_specs=[hbm] * 7,
        out_specs=pl.BlockSpec(memory_space=pltpu.VMEM),
        scratch_shapes=[
            vmem(rows, feats, dtype=BF16), vmem(rows, feats, dtype=BF16),
            vmem(rows, feats, dtype=BF16), vmem(rows, feats, dtype=BF16),
            vmem(rows, width), vmem(rows, width),
            vmem(rows, 2 * width, dtype=BF16), vmem(rows, width, dtype=BF16),
            vmem(rows, width, dtype=BF16), vmem(rows, width, dtype=BF16),
            vmem(rows, ranks), vmem(levels, ranks, ranks), vmem(levels + 1, ranks, ranks),
            vmem(width, ranks), vmem(width, ranks), vmem(width, ranks), vmem(half, ranks),
            vmem(half, ranks, dtype=BF16), vmem(half, ranks, dtype=BF16),
            vmem(half, ranks, dtype=BF16), vmem(2, half, ranks, dtype=BF16),
            vmem(half, ranks, dtype=BF16), vmem(3, half, ranks, dtype=BF16),
            vmem(5, half, ranks, dtype=BF16), vmem(half, ranks), vmem(half, ranks),
            vmem(rows, width, dtype=BF16), vmem(rows, width, dtype=BF16),
            vmem(rows, width),
            pltpu.SMEM((1, 4), jnp.int32), pltpu.SMEM((1,), jnp.int32),
            pltpu.SemaphoreType.DMA((7,)),
            pltpu.SemaphoreType.DMA((sends,)),
            pltpu.SemaphoreType.DMA((sends,)),
        ],
        compiler_params=pltpu.CompilerParams(
            collective_id=0, has_side_effects=True, vmem_limit_bytes=56 * 1024 * 1024),
    )(features, probes, bases, transfers[0], couplings[0], near_list, near_count)


def solution(mesh):
    in_specs = (
        P("leaf", None),
        P("leaf", None),
        P("leaf", None),
        P("leaf", None, None, None),
        P("leaf", None, None, None),
        P("leaf", None),
        P("leaf"),
    )
    return jax.shard_map(
        functools.partial(shards, mesh.shape["leaf"]),
        mesh=mesh, in_specs=in_specs, out_specs=P("leaf", None), check_vma=False)
```

```python
import functools

import jax
import jax.numpy as jnp
from jax import lax
from jax.experimental import pallas as pl
from jax.experimental.pallas import tpu as pltpu
from jax.sharding import PartitionSpec as P

F32, BF16 = jnp.float32, jnp.bfloat16
MESH = pl.DeviceIdType.MESH
CHUNKS = 16
BLOCKS = ((0, 256), (256, 128), (384, 128))
BURSTS = (5, 6, 7)

NN = (((1,), (0,)), ((), ()))
NT = (((1,), (1,)), ((), ()))
TN = (((0,), (0,)), ((), ()))


def dot(a, b, dims=NN):
    return lax.dot_general(a, b, dims, preferred_element_type=F32)


def split(a):
    high = a.astype(BF16)
    return high, (a - high.astype(F32)).astype(BF16)


def dot3(a, b, dims=NN):
    (ah, al), (bh, bl) = split(a), split(b)
    return dot(ah, bh, dims) + (dot(ah, bl, dims) + dot(al, bh, dims))


class Move:
    def __init__(self, copy, sends=None, receives=None):
        self.copy, self.sends, self.receives = copy, sends, receives

    @staticmethod
    def run(act, when):
        if when is None:
            act()
        else:
            pl.when(when)(act)

    def start(self, when=None):
        self.run(self.copy.start, self.sends if when is None else jnp.logical_and(self.sends, when))
        return self

    def wait_send(self):
        self.run(self.copy.wait_send, self.sends)

    def wait_recv(self):
        self.run(self.copy.wait_recv, self.receives)


def kernel(n, feat, prob, base, tran, coup, nlist_hbm, ncount_hbm, out,
           phi_q, phi_p, phi_g, phi_o, x_q, x_o, x_cat, x_b, x_p, x_g, u, tm, km,
           s0, s0_r, t1, t1_r, t2, t2_r, v3, v3_r, t4, ss, ss_r, e1, e1_r, bk, bk_r, acc, kept_h, kept_l,
           nlist, ncount, ld_sem, snd, rcv):
    me = lax.axis_index("leaf")
    core = lax.rem(me, 2)
    rows, feats = phi_q.shape
    ranks = u.shape[1]
    half = x_q.shape[1] // 2
    g = (3.0 / ranks) ** 0.5
    scale = 1.0 / (feats * rows)

    def flip(h):
        return (1 << h) - (2 << h) * lax.rem(me // (1 << h), 2)

    other = me + flip(0)
    source = me + 2 - 4 * core
    target = me - 2 + 4 * core
    has_source = jnp.logical_and(source >= 0, source < n)
    has_target = jnp.logical_and(target >= 0, target < n)
    next_chip, cross, cross_next = me + flip(1), me + flip(2), me + flip(1) + flip(2)
    level3 = me + flip(2) + flip(3)
    level4, level4_far = me + flip(4), me + flip(2) + flip(3) + flip(4)
    early = lax.rem(me // 2, 8) < 4
    late = jnp.logical_not(early)
    hurried = lax.rem(me, 16) == 0
    row_end = lax.rem(me // 2, 8) == 7

    barrier = pltpu.get_barrier_semaphore()

    def greet(p):
        pl.semaphore_signal(barrier, inc=1, device_id=(p,), device_id_type=MESH)

    fixed = (other, cross_next, level4_far, level3, cross, level4)
    pl.when(has_target)(lambda: greet(target))
    pl.when(has_source)(lambda: greet(source))
    for p in fixed:
        greet(p)

    def load(src, dst, at):
        copy = pltpu.make_async_copy(src, dst, ld_sem.at[at])
        copy.start()
        return copy

    ld_x = load(prob, x_q, 0)
    ld_u = load(base, u, 1)
    ld_t = load(tran, tm, 2)
    ld_phi = load(feat, phi_q, 3)
    ld_k = load(coup, km, 4)
    ld_list = load(nlist_hbm, nlist, 5)
    ld_count = load(ncount_hbm, ncount, 6)

    def member(offset):
        found = jnp.float32(0.0)
        for k in range(nlist.shape[1]):
            hit = jnp.logical_and(nlist[0, k] == me + offset, k < ncount[0])
            found = jnp.maximum(found, jnp.where(hit, 1.0, 0.0))
        return found

    def tile_of(a, b):
        gram = dot(a, b, NT)
        return split(gram * gram * scale)

    def apply_wide(th, tl, cat):
        wide = dot(th, cat)
        return wide[:, :2 * half] + (wide[:, 2 * half:] + dot(tl, cat[:, :2 * half]))

    def split_probes():
        ld_x.wait()
        xh, xl = split(x_q[...])
        x_b[...] = xh
        x_cat[:, :2 * half] = xh
        x_cat[:, 2 * half:] = xl

    def own():
        def step(k, carry):
            at = pl.ds(pl.multiple_of(k * 256, 256), 256)
            th, tl = tile_of(phi_q[at, :], phi_q[...])
            acc[at, :] += apply_wide(th, tl, x_cat[...])
            return carry

        lax.fori_loop(0, rows // 256, step, 0)

    acc[...] = jnp.zeros_like(acc)

    @pl.when(early)
    def _():
        split_probes()
        for ld in (ld_u, ld_t, ld_phi, ld_k):
            ld.wait()
        own()

    pl.semaphore_wait(barrier, len(fixed) + has_source.astype(jnp.int32) + has_target.astype(jnp.int32))

    count, sent = [0], []

    def move(src, dst, to, sends=None, receives=None):
        at = count[0]
        count[0] += 1
        return Move(pltpu.make_async_remote_copy(
            src_ref=src, dst_ref=dst, send_sem=snd.at[at], recv_sem=rcv.at[at],
            device_id=(to,), device_id_type=MESH), sends, receives)

    def send(*args):
        sent.append(move(*args).start())
        return sent[-1]

    def ahead(src, dst):
        return move(src, dst, target, has_target, has_source)

    def part(k, parts):
        return pl.ds(k * (rows // parts), rows // parts)

    phi_moves = [ahead(feat.at[part(k, CHUNKS)], phi_p.at[part(k, CHUNKS)]) for k in range(CHUNKS)]
    x_moves = [ahead(x_b.at[part(k, 2)], x_p.at[part(k, 2)]) for k in range(2)]
    waiting = phi_moves[:6] + x_moves + phi_moves[6:]

    def burst(stage):
        for k, m in enumerate(waiting):
            if sum(BURSTS[:stage]) <= k < sum(BURSTS[:stage + 1]):
                if stage == 0:
                    m.start()
                else:
                    m.start(jnp.logical_not(hurried))
        if stage == 0:
            for m in [m for m in waiting[BURSTS[0]:] if m not in x_moves] + x_moves:
                m.start(hurried)

    burst(0)
    o_moves = [send(feat.at[part(k, 2)], phi_o.at[part(k, 2)], other) for k in range(2)]
    xo_move = send(prob, x_o, other)

    @pl.when(jnp.logical_not(has_source))
    def _():
        phi_p[...] = jnp.zeros_like(phi_p)
        x_p[...] = jnp.zeros_like(x_p)

    @pl.when(jnp.logical_not(has_target))
    def _():
        bk_r[...] = jnp.zeros_like(bk_r)

    pl.when(late)(split_probes)

    pl.when(late)(ld_u.wait)
    s0[...] = dot3(x_q[...].T, u[...])
    pl.when(late)(ld_t.wait)
    t1[...] = (g * 2.0 ** -0.5) * dot3(s0[...], tm[0])
    keep = pl.multiple_of(half * core, half)
    give = pl.multiple_of(half - half * core, half)
    t1_move = send(t1.at[pl.ds(give, half)], t1_r, other)
    s0_move = send(s0, s0_r, other)

    ld_list.wait()
    ld_count.wait()
    m_p = member(2 - 4 * core)
    m_g = member(2 * core - 1)
    m_o = member(1 - 2 * core)
    m_b = member(4 * core - 2)

    def beside(k):
        if k == 0:
            xo_move.wait_recv()
        o_moves[k].wait_recv()
        th, tl = tile_of(phi_q[...], phi_o[part(k, 2), :])
        xoh, xol = split(x_o[part(k, 2), :])
        acc[...] += m_o * apply_wide(th, tl, jnp.concatenate([xoh, xol], axis=1))

    spans = [pl.ds(start, length) for start, length in BLOCKS]
    xg_move = move(x_p, x_g, other)
    fwd = [move(phi_p.at[at], phi_g.at[at], other) for at in spans]
    back = [move(bk.at[at], bk_r.at[at], source, has_source, has_target) for at in spans]

    def take_probes():
        for m in x_moves:
            m.wait_recv()
        xg_move.start()

    def kept_tiles():
        take_probes()
        xs = x_p[...]
        acc[...] += m_p * (dot(kept_h[...], xs, TN) + dot(kept_l[...], xs, TN))

    def far_pair(k):
        start, length = BLOCKS[k]
        at = spans[k]
        if k == 0:
            pl.when(jnp.logical_not(row_end))(take_probes)
        for m in phi_moves[start * CHUNKS // rows:(start + length) * CHUNKS // rows]:
            m.wait_recv()
        fwd[k].start()
        th, tl = tile_of(phi_p[at, :], phi_q[...])
        bk[at, :] = apply_wide(th, tl, x_cat[...]).astype(BF16)
        back[k].start()

        @pl.when(row_end)
        def _():
            kept_h[at, :] = th
            kept_l[at, :] = tl

        @pl.when(jnp.logical_not(row_end))
        def _():
            xs = x_p[at, :]
            acc[...] += m_p * (dot(th, xs, TN) + dot(tl, xs, TN))

    def near_pair(k):
        at = spans[k]
        if k == 0:
            xg_move.wait_recv()
        fwd[k].wait_recv()
        th, tl = tile_of(phi_q[...], phi_g[at, :])
        xs = x_g[at, :]
        acc[...] += m_g * (dot(th, xs) + dot(tl, xs))

    def factor(level):
        return g * 2.0 ** (-0.5 * level)

    t1_move.wait_recv()
    s1 = t1[pl.ds(keep, half), :] + t1_r[...]
    mine2 = factor(2) * dot3(s1, tm[1])
    t2[...] = mine2.astype(BF16)
    t2_move = send(t2, t2_r, next_chip)
    mine3 = factor(3) * dot3(mine2, tm[2])
    v3[...] = mine3.astype(BF16)
    v3_moves = [send(v3, v3_r.at[1], cross_next), send(v3, v3_r.at[0], cross)]
    ss[0] = s1.astype(BF16)
    s1_move = send(ss.at[0], ss_r.at[0], next_chip)
    burst(1)
    pl.when(late)(ld_phi.wait)
    beside(0)
    beside(1)

    t2_move.wait_recv()
    from2 = t2_r[...]
    ss[1] = (mine2 + from2.astype(F32)).astype(BF16)
    s2_move = send(ss.at[1], ss_r.at[1], cross)
    t2h, t2l = split(tm[2])
    mine3 = mine3 + factor(3) * (dot(from2, t2h) + dot(from2, t2l))
    pl.when(late)(ld_k.wait)
    s0_move.wait_recv()
    e0 = g * dot3(s0_r[...], km[0], NT)
    for m in v3_moves:
        m.wait_recv()
    s3 = mine3 + (v3_r[0].astype(F32) + v3_r[1].astype(F32))
    t4[...] = (factor(4) * dot3(s3, tm[3])).astype(BF16)
    t4_moves = [send(t4, ss_r.at[4], level4_far), send(t4, ss_r.at[3], level4)]
    ss[2] = s3.astype(BF16)
    s3_move = send(ss.at[2], ss_r.at[2], level3)
    burst(2)

    def couple(level, m):
        m.wait_recv()
        received = ss_r[level - 1]
        kh, kl = split(km[level])
        return g * (dot(received, kh, NT) + dot(received, kl, NT))

    coupled1 = couple(1, s1_move)
    far_pair(0)
    pl.when(jnp.logical_not(row_end))(lambda: near_pair(0))
    coupled2 = couple(2, s2_move)
    far_pair(1)

    @pl.when(row_end)
    def _():
        far_pair(2)
        kept_tiles()
        near_pair(0)

    for m in t4_moves:
        m.wait_recv()
    e = g * dot3(ss_r[3].astype(F32) + ss_r[4].astype(F32), km[4], NT)
    e = couple(3, s3_move) + factor(4) * dot3(e, tm[3], NT)
    e = coupled2 + factor(3) * dot3(e, tm[2], NT)
    e1[...] = coupled1 + factor(2) * dot3(e, tm[1], NT)
    e1_move = send(e1, e1_r, other)
    near_pair(1)
    pl.when(jnp.logical_not(row_end))(lambda: far_pair(2))
    e1_move.wait_recv()
    mine, theirs = e1[...], e1_r[...]
    first = jnp.where(core == 0, mine, theirs)
    second = jnp.where(core == 0, theirs, mine)
    e0 = e0 + factor(1) * dot3(jnp.concatenate([first, second], axis=0), tm[0], NT)
    acc[...] += dot3(u[...], e0, NT)
    near_pair(2)
    pl.when(late)(own)
    for m in back:
        m.wait_recv()
    out[...] = acc[...] + m_b * bk_r[...].astype(F32)
    for m in phi_moves + x_moves + fwd + back + [xg_move] + sent:
        m.wait_send()


def shards(n, features, probes, bases, transfers, couplings, near_list, near_count):
    rows, feats = features.shape
    width = probes.shape[1]
    half = width // 2
    ranks = bases.shape[1]
    levels = transfers.shape[1]
    sends = CHUNKS + 2 * len(BLOCKS) + 17
    hbm = pl.BlockSpec(memory_space=pltpu.HBM)

    def vmem(*shape, dtype=F32):
        return pltpu.VMEM(shape, dtype)

    return pl.pallas_call(
        functools.partial(kernel, n),
        out_shape=jax.ShapeDtypeStruct((rows, width), F32),
        in_specs=[hbm] * 7,
        out_specs=pl.BlockSpec(memory_space=pltpu.VMEM),
        scratch_shapes=[
            vmem(rows, feats, dtype=BF16), vmem(rows, feats, dtype=BF16),
            vmem(rows, feats, dtype=BF16), vmem(rows, feats, dtype=BF16),
            vmem(rows, width), vmem(rows, width),
            vmem(rows, 2 * width, dtype=BF16), vmem(rows, width, dtype=BF16),
            vmem(rows, width, dtype=BF16), vmem(rows, width, dtype=BF16),
            vmem(rows, ranks), vmem(levels, ranks, ranks), vmem(levels + 1, ranks, ranks),
            vmem(width, ranks), vmem(width, ranks), vmem(width, ranks), vmem(half, ranks),
            vmem(half, ranks, dtype=BF16), vmem(half, ranks, dtype=BF16),
            vmem(half, ranks, dtype=BF16), vmem(2, half, ranks, dtype=BF16),
            vmem(half, ranks, dtype=BF16), vmem(3, half, ranks, dtype=BF16),
            vmem(5, half, ranks, dtype=BF16), vmem(half, ranks), vmem(half, ranks),
            vmem(rows, width, dtype=BF16), vmem(rows, width, dtype=BF16),
            vmem(rows, width), vmem(rows, rows, dtype=BF16), vmem(rows, rows, dtype=BF16),
            pltpu.SMEM((1, 4), jnp.int32), pltpu.SMEM((1,), jnp.int32),
            pltpu.SemaphoreType.DMA((7,)),
            pltpu.SemaphoreType.DMA((sends,)),
            pltpu.SemaphoreType.DMA((sends,)),
        ],
        compiler_params=pltpu.CompilerParams(
            collective_id=0, has_side_effects=True, vmem_limit_bytes=56 * 1024 * 1024),
    )(features, probes, bases, transfers[0], couplings[0], near_list, near_count)


def solution(mesh):
    in_specs = (
        P("leaf", None),
        P("leaf", None),
        P("leaf", None),
        P("leaf", None, None, None),
        P("leaf", None, None, None),
        P("leaf", None),
        P("leaf"),
    )
    return jax.shard_map(
        functools.partial(shards, mesh.shape["leaf"]),
        mesh=mesh, in_specs=in_specs, out_specs=P("leaf", None), check_vma=False)
```
